32 devices in a mesh: ctx: 16 (over z, y, x), ch: 2 (over core).
Axes of the slice: x: 2, y: 2, z: 4, core: 2. Of those that a mesh axis runs over, the one named last changes fastest.
Arguments:
- value_in: bfloat16 [2048, 4096], P('ctx', 'ch'), may hold values from -6 to 6
- key_in: bfloat16 [2048, 4096], P('ctx', 'ch'), may hold values from -6 to 6
- gate_short: bfloat16 [2048, 4096], P('ctx', 'ch'), may hold values from -6 to 6
- gate_long: bfloat16 [2048, 4096], P('ctx', 'ch'), may hold values from -6 to 6
- short_filter: bfloat16 [256, 128], P('ch'), may hold values from -0.5 to 0.5
- long_filter: float32 [4096, 2048], P(('ch', 'ctx')), may hold values from -2 to 2
- skip_gain: float32 [4096], P('ch'), may hold values from 0.5 to 1.5
- out_weight: bfloat16 [4096, 4096], P('ctx', 'ch'), may hold values from -0.09375 to 0.09375
Outputs:
- layer_out: bfloat16 [2048, 4096], P('ctx', 'ch')
The draws below stay inside these ranges and needn't reach their ends.
All inputs are finite; a program needn't handle non-finite values.
Results may differ from the reference program's by a relative error of at most 0.0067.
Values may be sent and summed in bfloat16 or wider, within the bound.
A program may use at most 64 MiB of HBM per device.

```python
import jax
import jax.numpy as jnp
from jax import lax

MODEL_WIDTH = 4096
GSIZE = 16
TAPS = 128
SEQUENCE_TOKENS = 2048
GROUPS = 256


def draw_long_filter(key, part):
    random_subkeys = jax.random.split(jax.random.fold_in(key, 17), 8)
    delay_offsets = jnp.arange(SEQUENCE_TOKENS, dtype=jnp.float32)
    fast_share = 0.3
    quick_mask = jax.random.uniform(random_subkeys[0], (MODEL_WIDTH,)) < fast_share
    quick_rate = jnp.exp(jax.random.uniform(random_subkeys[1], (MODEL_WIDTH,), minval=jnp.log(1.0 / 50.0), maxval=jnp.log(1.0 / 30.0)))
    steady_rate = jnp.exp(jax.random.uniform(random_subkeys[2], (MODEL_WIDTH,), minval=jnp.log(0.1 / SEQUENCE_TOKENS), maxval=jnp.log(1.0 / SEQUENCE_TOKENS)))
    decay_rate = jnp.where(quick_mask, quick_rate, steady_rate)
    decay_profile = jnp.exp(-decay_rate[:, None] * delay_offsets[None, :])
    for spike_pulse in range(2):
        spike_position = jax.random.randint(random_subkeys[3 + spike_pulse], (MODEL_WIDTH, 1), 1, SEQUENCE_TOKENS).astype(jnp.float32)
        spike_retained = jax.random.uniform(random_subkeys[5 + spike_pulse], (MODEL_WIDTH, 1), minval=0.6, maxval=0.85)
        decay_profile = decay_profile * jnp.where(delay_offsets[None, :] >= spike_position, spike_retained, 1.0)
    jitter = jnp.clip(jax.random.normal(random_subkeys[7], (MODEL_WIDTH, SEQUENCE_TOKENS)), -4.0, 4.0)
    norm_scale = 1.0 / jnp.sqrt(jnp.sum(decay_profile * decay_profile, axis=1, keepdims=True))
    return (jitter * decay_profile * norm_scale).astype(jnp.float32)


def level_of(own_key, shape, shards, least, top_value):
    level, own = 1.0, jax.random.fold_in(own_key, 6)
    for axis_at, parts in shards:
        draws = jnp.exp(jax.random.uniform(jax.random.fold_in(own, axis_at), (parts,), jnp.float32, least / len(shards), top_value / len(shards)))
        level = level * jnp.repeat(draws, shape[axis_at] // parts).reshape([-1 if axis == axis_at else 1 for axis in range(len(shape))])
    return level


def centred(own_key, shape, scale, limit, pieces=(), held_as=jnp.bfloat16):
    array = scale * jax.random.normal(own_key, shape, jnp.float32)
    if pieces:
        array = array * level_of(own_key, shape, pieces, -0.22, 0.18)
    return jnp.clip(array, -limit, limit).astype(held_as)


def setup_inputs(seed: int = 0) -> dict:
    splits = jax.random.split(jax.random.key(seed), 9)
    value_in = centred(splits[0], (SEQUENCE_TOKENS, MODEL_WIDTH), 1.0, 6.0, ((0, 16), (1, 2)))
    key_in = centred(splits[1], (SEQUENCE_TOKENS, MODEL_WIDTH), 1.0, 6.0, ((0, 16), (1, 2)))
    gate_short = centred(splits[2], (SEQUENCE_TOKENS, MODEL_WIDTH), 1.0, 6.0, ((0, 16), (1, 2)))
    gate_long = centred(splits[3], (SEQUENCE_TOKENS, MODEL_WIDTH), 1.0, 6.0, ((0, 16), (1, 2)))
    short_filter = centred(splits[4], (GROUPS, TAPS), TAPS ** -0.5, 0.5, ((0, 2),))
    long_filter = draw_long_filter(jax.random.fold_in(splits[8], 71), 0)
    skip_gain = jnp.clip(0.5 + 1.0 * jax.random.uniform(splits[6], (MODEL_WIDTH,), jnp.float32) ** level_of(splits[6], (MODEL_WIDTH,), ((0, 2),), -0.2, 0.2), 0.5, 1.5)
    out_weight = centred(splits[7], (MODEL_WIDTH, MODEL_WIDTH), MODEL_WIDTH ** -0.5, 0.09375, ((0, 16), (1, 2)))
    return {"value_in": value_in, "key_in": key_in, "gate_short": gate_short, "gate_long": gate_long, "short_filter": short_filter, "long_filter": long_filter, "skip_gain": skip_gain, "out_weight": out_weight}


def reference(value_in, key_in, gate_short, gate_long, short_filter, long_filter, skip_gain, out_weight):
    product = (value_in.astype(jnp.float32) * key_in.astype(jnp.float32)).astype(jnp.bfloat16)
    tap_table = jnp.repeat(short_filter.astype(jnp.float32), GSIZE, axis=0).T
    padded = jnp.concatenate([jnp.zeros((TAPS - 1, MODEL_WIDTH), jnp.float32), product.astype(jnp.float32)], 0)

    def add_tap(tap_index, total):
        where_at = jnp.asarray(tap_index).astype(jnp.int32)
        start = (TAPS - 1 - where_at).astype(jnp.int32)
        piece = lax.dynamic_slice_in_dim(padded, start, SEQUENCE_TOKENS, 0)
        weights = lax.dynamic_index_in_dim(tap_table, where_at, 0, keepdims=False)
        return total + weights[None, :] * piece

    short_out = lax.fori_loop(0, TAPS, add_tap, jnp.zeros((SEQUENCE_TOKENS, MODEL_WIDTH), jnp.float32))
    mid_rows = (gate_short.astype(jnp.float32) * short_out).astype(jnp.bfloat16)
    span_len = 2 * SEQUENCE_TOKENS
    block_size = min(64, MODEL_WIDTH)

    def block_conv(pair):
        signal, filters = pair
        spectra = jnp.fft.rfft(signal, n=span_len, axis=-1) * jnp.fft.rfft(filters, n=span_len, axis=-1)
        return jnp.fft.irfft(spectra, n=span_len, axis=-1)[:, :SEQUENCE_TOKENS].astype(jnp.float32)

    signals = mid_rows.astype(jnp.float32).T.reshape(MODEL_WIDTH // block_size, block_size, SEQUENCE_TOKENS)
    filters = long_filter.astype(jnp.float32).reshape(MODEL_WIDTH // block_size, block_size, SEQUENCE_TOKENS)
    long_out = lax.map(block_conv, (signals, filters)).reshape(MODEL_WIDTH, SEQUENCE_TOKENS).T.astype(jnp.bfloat16)
    gated = (gate_long.astype(jnp.float32) * (long_out.astype(jnp.float32) + skip_gain.astype(jnp.float32)[None, :] * mid_rows.astype(jnp.float32))).astype(jnp.bfloat16)
    return jnp.dot(gated, out_weight, preferred_element_type=jnp.float32).astype(jnp.bfloat16)
```

```python
import functools

import jax
import jax.numpy as jnp
from jax import lax
from jax.experimental import pallas as pl
from jax.experimental.pallas import tpu as pltpu
from jax.sharding import PartitionSpec as P


def short_kernel(group_size, own_ref, prior_ref, gate_ref, taps_ref, mid_ref):
    rows, lanes = own_ref.shape
    tap_count = taps_ref.shape[1]
    row_at = lax.broadcasted_iota(jnp.int32, (rows, tap_count), 0)
    lane_at = lax.broadcasted_iota(jnp.int32, (rows, tap_count), 1)
    before = lane_at > row_at
    window = jnp.concatenate([prior_ref[...], own_ref[...]], 0)
    group_at = lax.broadcasted_iota(jnp.int32, (rows, lanes), 1) // group_size
    total = jnp.zeros((rows, lanes), jnp.float32)
    for group in range(lanes // group_size):
        line = jnp.broadcast_to(taps_ref[group : group + 1, :], (rows, tap_count))
        turned = pltpu.roll(line, 0, 1, stride=1, stride_axis=0)
        band = jnp.concatenate(
            [jnp.where(before, turned, 0.0), jnp.where(before, 0.0, turned)], 1
        ).astype(jnp.bfloat16)
        part = jnp.dot(band, window, preferred_element_type=jnp.float32)
        total = jnp.where(group_at == group, part, total)
    mid = gate_ref[...].astype(jnp.float32) * total
    mid_ref[...] = mid.T.astype(jnp.bfloat16)


def short_conv(product, prior, gate_short, short_filter):
    rows, channels = product.shape
    groups, tap_count = short_filter.shape
    group_size = channels // groups
    lanes = min(128, channels)
    taps = jnp.roll(short_filter[:, ::-1], 1, axis=1).astype(jnp.float32)
    block = pl.BlockSpec((rows, lanes), lambda i: (0, i))
    return pl.pallas_call(
        functools.partial(short_kernel, group_size),
        grid=(channels // lanes,),
        in_specs=[block, block, block, pl.BlockSpec((lanes // group_size, tap_count), lambda i: (i, 0))],
        out_specs=pl.BlockSpec((lanes, rows), lambda i: (i, 0)),
        out_shape=jax.ShapeDtypeStruct((channels, rows), jnp.bfloat16),
        cost_estimate=pl.CostEstimate(
            flops=4 * groups * rows * tap_count * lanes, bytes_accessed=8 * rows * channels, transcendentals=0
        ),
        name="short_conv",
    )(product, prior, gate_short, taps)


def long_kernel(x_ref, h_ref, gate_ref, skip_ref, out_ref):
    batch, blocks, width = x_ref.shape
    half = width // 2
    row_at = lax.broadcasted_iota(jnp.int32, (half, width), 0)
    lane_at = lax.broadcasted_iota(jnp.int32, (half, width), 1)
    after = lane_at >= row_at
    low = lax.broadcasted_iota(jnp.int32, (blocks, width), 1) < half
    first = lax.broadcasted_iota(jnp.int32, (blocks, width), 0) < 1
    deep_at = lax.broadcasted_iota(jnp.int32, (2 * batch, blocks, width), 1)
    signals = [x_ref[c].astype(jnp.float32) for c in range(batch)]
    pieces = []
    zero = jnp.zeros((blocks, width), jnp.float32)
    for c in range(batch):
        swapped = pltpu.roll(signals[c], half, 1)
        even = signals[c] if c % 2 == 0 else swapped
        odd = swapped if c % 2 == 0 else signals[c]
        keep = low if c % 2 == 0 else jnp.logical_not(low)
        for piece in (even, odd):
            spread = [zero] * (batch // 2)
            spread[c // 2] = jnp.where(keep, piece, 0.0)
            pieces.append(jnp.concatenate(spread, 1))
    left = jnp.concatenate(pieces, 0).astype(jnp.bfloat16)
    filters = [h_ref[c].astype(jnp.float32) for c in range(batch)]
    previous = [jnp.zeros((half, width), jnp.float32)] * batch
    total = jnp.zeros((2 * batch, blocks, width), jnp.float32)
    for p in range(blocks):
        rows = []
        for c in range(batch):
            line = jnp.broadcast_to(filters[c][p : p + 1, :], (half, width))
            turned = pltpu.roll(line, 0, 1, stride=1, stride_axis=0)
            rows.append(jnp.where(after, turned, previous[c]))
            previous[c] = turned
        right = jnp.concatenate(rows, 0).astype(jnp.bfloat16)
        part = jnp.dot(left, right, preferred_element_type=jnp.float32)
        part = part.reshape(2 * batch, blocks, width)
        if p:
            part = jnp.where(deep_at >= p, pltpu.roll(part, p, 1), 0.0)
        total = total + part
    for c in range(batch):
        even, odd = total[2 * c], total[2 * c + 1]
        later = jnp.where(first, 0.0, pltpu.roll(odd, 1, 0))
        result = even + pltpu.roll(jnp.where(low, odd, later), half, 1)
        result = result.astype(jnp.bfloat16).astype(jnp.float32)
        gain = jnp.broadcast_to(skip_ref[c], (blocks, width))
        out_ref[c] = (gate_ref[c].astype(jnp.float32) * (result + gain * signals[c])).astype(jnp.bfloat16)


def long_conv(signals, filters, gates, gains):
    channels, blocks, width = signals.shape
    batch = 4
    block = pl.BlockSpec((batch, blocks, width), lambda i: (i, 0, 0))
    wide_gain = jnp.broadcast_to(gains[:, None, None], (channels, 1, width))
    return pl.pallas_call(
        long_kernel,
        grid=(channels // batch,),
        in_specs=[block, block, block, pl.BlockSpec((batch, 1, width), lambda i: (i, 0, 0))],
        out_specs=block,
        out_shape=jax.ShapeDtypeStruct(signals.shape, jnp.bfloat16),
        cost_estimate=pl.CostEstimate(
            flops=4 * channels * blocks * blocks * width * width,
            bytes_accessed=8 * channels * blocks * width,
            transcendentals=0,
        ),
        name="long_conv",
    )(signals, filters, gates, wide_gain)


def shards(
    value_in, key_in, gate_short, gate_long, short_filter, long_filter, skip_gain, out_weight
):
    tok_rows, channels = value_in.shape
    ctx_ways, ch_ways = lax.axis_size("ctx"), lax.axis_size("ch")
    per_dev = channels // ctx_ways
    inner = 2 ** ((ctx_ways.bit_length() - 1) // 2)
    outer = ctx_ways // inner
    lines = [[inner * m + g for m in range(outer)] for g in range(inner)]
    planes = [[inner * m + g for g in range(inner)] for m in range(outer)]
    owned = [
        ch_ways * (inner * (m // ch_ways) + g) + m % ch_ways for m in range(outer) for g in range(inner)
    ]

    def spread(by_channel):
        blocks = by_channel.reshape(outer // ch_ways, inner, ch_ways, per_dev, tok_rows)
        blocks = blocks.transpose(0, 2, 1, 3, 4).reshape(ctx_ways, per_dev, tok_rows)
        sent = lax.all_to_all(blocks, "ctx", split_axis=0, concat_axis=0, tiled=True)
        return sent.transpose(1, 0, 2)

    weights = lax.all_gather(out_weight, "ctx", axis=0, tiled=True, axis_index_groups=lines)
    product = (value_in.astype(jnp.float32) * key_in.astype(jnp.float32)).astype(jnp.bfloat16)
    prior = lax.ppermute(product, "ctx", [(s, s + 1) for s in range(ctx_ways - 1)])
    filters = lax.ppermute(
        long_filter.astype(jnp.bfloat16), "ctx", [(source, at) for at, source in enumerate(owned)]
    ).reshape(per_dev, ctx_ways, tok_rows)
    gates = spread(gate_long.T)
    signals = spread(short_conv(product, prior, gate_short, short_filter))
    me = lax.axis_index("ctx")
    line_at, place = me // inner, me % inner
    own_block = ch_ways * (inner * (line_at // ch_ways) + place) + line_at % ch_ways
    gains = lax.dynamic_slice_in_dim(skip_gain, own_block * per_dev, per_dev)
    gated = long_conv(signals, filters, gates, gains).transpose(1, 0, 2)
    gated = lax.all_to_all(
        gated.reshape(outer, inner, per_dev, tok_rows),
        "ctx",
        split_axis=0,
        concat_axis=0,
        axis_index_groups=lines,
        tiled=True,
    )
    gated = lax.all_gather(gated, "ch", axis=0, tiled=False)
    features = gated.transpose(2, 4, 0, 1, 3).reshape(inner * tok_rows, ch_ways * outer * per_dev)
    partial = jnp.dot(features, weights, preferred_element_type=jnp.float32).astype(jnp.bfloat16)
    partial = lax.all_to_all(
        partial.reshape(inner, tok_rows, channels),
        "ctx",
        split_axis=0,
        concat_axis=0,
        axis_index_groups=planes,
        tiled=True,
    )
    return partial.astype(jnp.float32).sum(0).astype(jnp.bfloat16)


def solution(mesh):
    in_specs = (
        P("ctx", "ch"),
        P("ctx", "ch"),
        P("ctx", "ch"),
        P("ctx", "ch"),
        P("ch", None),
        P(("ch", "ctx"), None),
        P("ch"),
        P("ctx", "ch"),
    )
    out_specs = P("ctx", "ch")
    return jax.shard_map(shards, mesh=mesh, in_specs=in_specs, out_specs=out_specs, check_vma=False)
```

```python
import functools

import jax
import jax.numpy as jnp
from jax import lax
from jax.experimental import pallas as pl
from jax.experimental.pallas import tpu as pltpu
from jax.sharding import PartitionSpec as P

MESH = pl.DeviceIdType.MESH
F32, BF16 = jnp.float32, jnp.bfloat16


def remote(src, dst, send_sem, recv_sem, ctx, ch=None):
    ch = lax.axis_index("ch") if ch is None else ch
    return pltpu.make_async_remote_copy(
        src_ref=src, dst_ref=dst, send_sem=send_sem, recv_sem=recv_sem, device_id=(ctx, ch), device_id_type=MESH
    )


def short_tile(group_size, own, prior, gate, taps_ref, first_group):
    rows, lanes = own.shape
    tap_count = taps_ref.shape[2]
    row_at = lax.broadcasted_iota(jnp.int32, (rows, tap_count), 0)
    lane_at = lax.broadcasted_iota(jnp.int32, (rows, tap_count), 1)
    before = lane_at > row_at
    window = jnp.concatenate([prior, own], 0)
    group_at = lax.broadcasted_iota(jnp.int32, (rows, lanes), 1) // group_size
    total = jnp.zeros((rows, lanes), F32)
    for group in range(lanes // group_size):
        line = jnp.broadcast_to(taps_ref[first_group + group], (rows, tap_count))
        turned = pltpu.roll(line, 0, 1, stride=1, stride_axis=0)
        band = jnp.concatenate([jnp.where(before, turned, 0.0), jnp.where(before, 0.0, turned)], 1).astype(BF16)
        part = jnp.dot(band, window, preferred_element_type=F32)
        total = jnp.where(group_at == group, part, total)
    return (gate.astype(F32) * total).T


def long_quad(batch, start, xs, hs, gs, skip_ref, skip_at, out):
    _, blocks, width = xs.shape
    half = width // 2
    row_at = lax.broadcasted_iota(jnp.int32, (half, width), 0)
    lane_at = lax.broadcasted_iota(jnp.int32, (half, width), 1)
    after = lane_at >= row_at
    low = lax.broadcasted_iota(jnp.int32, (blocks, width), 1) < half
    first = lax.broadcasted_iota(jnp.int32, (blocks, width), 0) < 1
    deep_at = lax.broadcasted_iota(jnp.int32, (2 * batch, blocks, width), 1)
    signals = [xs[start + c] for c in range(batch)]
    pieces = []
    zero = jnp.zeros((blocks, width), F32)
    for c in range(batch):
        swapped = pltpu.roll(signals[c], half, 1)
        even = signals[c] if c % 2 == 0 else swapped
        odd = swapped if c % 2 == 0 else signals[c]
        keep = low if c % 2 == 0 else jnp.logical_not(low)
        for piece in (even, odd):
            spread = [zero] * (batch // 2)
            spread[c // 2] = jnp.where(keep, piece, 0.0)
            pieces.append(jnp.concatenate(spread, 1))
    left = jnp.concatenate(pieces, 0).astype(BF16)
    previous = [jnp.zeros((half, width), F32)] * batch
    total = jnp.zeros((2 * batch, blocks, width), F32)
    for p in range(blocks):
        rows = []
        for c in range(batch):
            line = jnp.broadcast_to(hs[start + c, :, p * width : (p + 1) * width], (half, width))
            turned = pltpu.roll(line, 0, 1, stride=1, stride_axis=0)
            rows.append(jnp.where(after, turned, previous[c]))
            previous[c] = turned
        right = jnp.concatenate(rows, 0).astype(BF16)
        part = jnp.dot(left, right, preferred_element_type=F32)
        part = part.reshape(2 * batch, blocks, width)
        if p:
            part = jnp.where(deep_at >= p, pltpu.roll(part, p, 1), 0.0)
        total = total + part
    for c in range(batch):
        even, odd = total[2 * c], total[2 * c + 1]
        later = jnp.where(first, 0.0, pltpu.roll(odd, 1, 0))
        result = even + pltpu.roll(jnp.where(low, odd, later), half, 1)
        result = result.astype(BF16).astype(F32)
        gain = jnp.broadcast_to(skip_ref[skip_at + start + c], (blocks, width))
        out[start + c] = gs[start + c] * (result + gain * signals[c])


def kernel(
    sizes,
    value_ref, key_ref, gate_s_ref, gate_l_ref, taps_ref, filt_ref, skip_ref, w_ref,
    out_ref,
    prod, prior, mid_send, gate_send, filt_send, mid_in, gate_in, filt_in, gated, feat, wbuf,
    part_send, part_in, own_part, xs, hs, gs, ys,
    halo_sem, filt_sem, mid_s, mid_r, gate_s, gate_r, feat_s, feat_r, w_own, w_right, w_left, w_recv, part_s, part_r,
):
    ctx_ways, ch_ways, outer, inner, per_dev, group_size = sizes
    rows, channels = value_ref.shape
    me, core = lax.axis_index("ctx"), lax.axis_index("ch")
    line_at, place = me // inner, me % inner

    def owned(d):
        m, g = d // inner, d % inner
        return ch_ways * (inner * (m // ch_ways) + g) + m % ch_ways

    def owner_of(block):
        m_hi, g, e = block // (ch_ways * inner), (block // ch_ways) % inner, block % ch_ways
        return inner * (ch_ways * m_hi + e) + g

    barrier = pltpu.get_barrier_semaphore()

    @pl.loop(1, ctx_ways)
    def _(s):
        pl.semaphore_signal(barrier, inc=1, device_id=((me + s) % ctx_ways, core), device_id_type=MESH)

    for other in range(1, ch_ways):

        @pl.loop(0, outer)
        def _(m):
            pl.semaphore_signal(
                barrier, inc=1, device_id=(m * inner + place, (core + other) % ch_ways), device_id_type=MESH
            )

    prod[...] = (value_ref[...].astype(F32) * key_ref[...].astype(F32)).astype(BF16)
    filt_send[...] = filt_ref[...].astype(BF16)
    pl.semaphore_wait(barrier, ctx_ways - 1 + (ch_ways - 1) * outer)

    halo = remote(prod, prior, halo_sem.at[0], halo_sem.at[1], (me + 1) % ctx_ways)

    @pl.when(me < ctx_ways - 1)
    def _():
        halo.start()

    filt_to = owner_of(me)
    filt_copy = remote(filt_send, filt_in, filt_sem.at[0], filt_sem.at[1], filt_to)

    @pl.when(filt_to != me)
    def _():
        filt_copy.start()

    own_w = pltpu.make_async_copy(w_ref, wbuf.at[line_at], w_own)
    own_w.start()

    def right_copy(s):
        at = jnp.maximum(line_at - s, 0)
        src = w_ref if s == 0 else wbuf.at[at]
        return remote(src, wbuf.at[at], w_right.at[s], w_recv.at[at], (me + inner) % ctx_ways)

    def left_copy(s):
        at = jnp.minimum(line_at + s, outer - 1)
        src = w_ref if s == 0 else wbuf.at[at]
        return remote(src, wbuf.at[at], w_left.at[s], w_recv.at[at], (me + ctx_ways - inner) % ctx_ways)

    def right_on(s):
        return jnp.logical_and(line_at >= s, line_at < outer - 1)

    def left_on(s):
        return jnp.logical_and(line_at + s < outer, line_at > 0)

    def w_step(s):
        @pl.when(right_on(s))
        def _():
            copy = right_copy(s)
            if s:
                copy.wait_recv()
            copy.start()

        @pl.when(left_on(s))
        def _():
            copy = left_copy(s)
            if s:
                copy.wait_recv()
            copy.start()

    w_step(0)

    lanes = min(128, channels)
    in_tile = lanes // per_dev
    tiles = channels // lanes

    def block_copy(buf, into, send, recv, block):
        return remote(buf.at[block], into.at[me], send.at[block], recv.at[me], owner_of(block))

    def send_tile(tile, values, buf, into, send, recv):
        buf[pl.ds(tile * in_tile, in_tile)] = values.reshape(in_tile, per_dev, rows).astype(BF16)
        for b in range(in_tile):
            block = tile * in_tile + b

            @pl.when(owner_of(block) != me)
            def _():
                block_copy(buf, into, send, recv, block).start()

    shift = owned(me) // in_tile

    @pl.loop(0, tiles)
    def _(t):
        tile = (t + shift + 1) % tiles
        at = pl.ds(pl.multiple_of(tile * lanes, lanes), lanes)
        send_tile(tile, gate_l_ref[:, at].astype(F32).T, gate_send, gate_in, gate_s, gate_r)

    @pl.when(me > 0)
    def _():
        halo.wait_recv()

    @pl.when(me == 0)
    def _():
        prior[...] = jnp.zeros_like(prior)

    @pl.loop(0, tiles)
    def _(t):
        tile = (t + shift + 1) % tiles
        at = pl.ds(pl.multiple_of(tile * lanes, lanes), lanes)
        groups = lanes // group_size
        values = short_tile(group_size, prod[:, at], prior[:, at], gate_s_ref[:, at], taps_ref, tile * groups)
        send_tile(tile, values, mid_send, mid_in, mid_s, mid_r)

    if outer > 2:
        w_step(1)

    mine = owned(me)
    gate_in[me] = gate_send[mine]
    mid_in[me] = mid_send[mine]

    @pl.when(filt_to != me)
    def _():
        filt_copy.wait_recv()

    @pl.when(filt_to == me)
    def _():
        filt_in[...] = filt_send[...]

    @pl.loop(1, ctx_ways)
    def _(s):
        a = (me + s) % ctx_ways
        remote(gate_send.at[0], gate_in.at[a], gate_s.at[0], gate_r.at[a], a).wait_recv()
        remote(mid_send.at[0], mid_in.at[a], mid_s.at[0], mid_r.at[a], a).wait_recv()

    step, batch = xs.shape[0], 4

    def long_step(i):
        at = pl.ds(pl.multiple_of(i * step, step), step)
        xs[...] = jnp.swapaxes(mid_in[:, at, :].astype(F32), 0, 1)
        gs[...] = jnp.swapaxes(gate_in[:, at, :].astype(F32), 0, 1)
        hs[...] = filt_in[at, :].astype(F32).reshape(hs.shape)

        @pl.loop(0, step // batch)
        def _(q):
            long_quad(batch, q * batch, xs, hs, gs, skip_ref, i * step, ys)

        gated[:, at, :] = jnp.swapaxes(ys[...], 0, 1).astype(BF16)

    long_steps = per_dev // step
    for s in range(2, outer - 1):
        low, high = (s - 2) * long_steps // (outer - 2), (s - 1) * long_steps // (outer - 2)

        @pl.loop(low, high)
        def _(i):
            long_step(i)

        w_step(s)

    done = (max(outer - 3, 0)) * long_steps // max(outer - 2, 1)

    @pl.loop(done, long_steps)
    def _(i):
        long_step(i)

    slot = core * outer + line_at

    def feat_copy(m, ch, n):
        return remote(
            gated.at[pl.ds(m * inner, inner)], feat.at[slot], feat_s.at[n], feat_r.at[slot], m * inner + place, ch
        )

    for k in range(ch_ways):

        @pl.loop(0, outer)
        def _(s):
            m, ch = (line_at + s) % outer, (core + k) % ch_ways

            @pl.when(jnp.logical_or(m != line_at, ch != core))
            def _():
                feat_copy(m, ch, ch * outer + m).start()

    feat[slot] = gated[pl.ds(me - place, inner)]

    own_w.wait()
    for s in range(1, outer):

        @pl.when(jnp.logical_and(line_at == outer - 1, line_at >= s))
        def _():
            right_copy(s).wait_recv()

        @pl.when(jnp.logical_and(line_at == 0, line_at + s < outer))
        def _():
            left_copy(s).wait_recv()

    @pl.loop(0, ch_ways * outer)
    def _(n):
        @pl.when(n != slot)
        def _():
            remote(
                gated.at[pl.ds(0, inner)], feat.at[n], feat_s.at[n], feat_r.at[n], (n % outer) * inner + place, n // outer
            ).wait_recv()

    depth = ch_ways * outer * per_dev

    def features(g):
        return feat[:, g].astype(F32).reshape(depth, rows).T.astype(BF16)

    cols = min(512, channels)

    @pl.loop(1, inner)
    def _(s):
        g = (place + s) % inner
        left = features(g)

        @pl.loop(0, channels // cols)
        def _(n):
            at = pl.ds(pl.multiple_of(n * cols, cols), cols)
            right = wbuf[:, :, at].reshape(depth, cols)
            part_send[g, :, at] = jnp.dot(left, right, preferred_element_type=F32).astype(BF16)

        remote(part_send.at[g], part_in.at[place], part_s.at[g], part_r.at[place], me - place + g).start()

    left = features(place)

    @pl.loop(0, channels // cols)
    def _(n):
        at = pl.ds(pl.multiple_of(n * cols, cols), cols)
        right = wbuf[:, :, at].reshape(depth, cols)
        own_part[:, at] = jnp.dot(left, right, preferred_element_type=F32)

    @pl.loop(1, inner)
    def _(s):
        g = (place + s) % inner
        remote(part_send.at[g], part_in.at[g], part_s.at[g], part_r.at[g], me - place + g).wait_recv()

        own_part[...] += part_in[g].astype(F32)

    out_ref[...] = own_part[...].astype(BF16)

    @pl.when(me < ctx_ways - 1)
    def _():
        halo.wait_send()

    @pl.when(filt_to != me)
    def _():
        filt_copy.wait_send()

    for s in range(outer - 1):

        @pl.when(right_on(s))
        def _():
            right_copy(s).wait_send()

        @pl.when(left_on(s))
        def _():
            left_copy(s).wait_send()

    @pl.loop(0, ctx_ways)
    def _(block):
        @pl.when(owner_of(block) != me)
        def _():
            block_copy(gate_send, gate_in, gate_s, gate_r, block).wait_send()
            block_copy(mid_send, mid_in, mid_s, mid_r, block).wait_send()

    @pl.loop(0, ch_ways * outer)
    def _(n):
        @pl.when(n != slot)
        def _():
            feat_copy(n % outer, n // outer, n).wait_send()

    @pl.loop(1, inner)
    def _(s):
        g = (place + s) % inner
        remote(part_send.at[g], part_in.at[place], part_s.at[g], part_r.at[place], me - place + g).wait_send()


def shards(
    value_in, key_in, gate_short, gate_long, short_filter, long_filter, skip_gain, out_weight
):
    rows, channels = value_in.shape
    ctx_ways, ch_ways = lax.axis_size("ctx"), lax.axis_size("ch")
    per_dev = channels // ctx_ways
    inner = 2 ** ((ctx_ways.bit_length() - 1) // 2)
    outer = ctx_ways // inner
    group_size = channels // short_filter.shape[0]
    taps = jnp.roll(short_filter[:, ::-1], 1, axis=1).astype(F32)[:, None, :]
    me = lax.axis_index("ctx")
    line_at, place = me // inner, me % inner
    own_block = ch_ways * (inner * (line_at // ch_ways) + place) + line_at % ch_ways
    gains = lax.dynamic_slice_in_dim(skip_gain, own_block * per_dev, per_dev)
    gains = jnp.broadcast_to(gains[:, None, None], (per_dev, 1, rows))
    step = min(16, per_dev)
    seq_len = ctx_ways * rows
    sizes = (ctx_ways, ch_ways, outer, inner, per_dev, group_size)
    blocks = pltpu.VMEM((ctx_ways, per_dev, rows), BF16)
    tokens = pltpu.VMEM((rows, channels), BF16)
    filt = pltpu.VMEM((per_dev, seq_len), BF16)
    lines = pltpu.VMEM((step, ctx_ways, rows), F32)
    dma = pltpu.SemaphoreType.DMA
    vmem = pl.BlockSpec(memory_space=pltpu.VMEM)
    return pl.pallas_call(
        functools.partial(kernel, sizes),
        out_shape=jax.ShapeDtypeStruct((rows, channels), BF16),
        in_specs=[vmem] * 7 + [pl.BlockSpec(memory_space=pl.ANY)],
        out_specs=vmem,
        scratch_shapes=[
            tokens, tokens, blocks, blocks, filt, blocks, blocks, filt, blocks,
            pltpu.VMEM((ch_ways * outer, inner, per_dev, rows), BF16),
            pltpu.VMEM((outer,) + out_weight.shape, BF16),
            pltpu.VMEM((inner, rows, channels), BF16),
            pltpu.VMEM((inner, rows, channels), BF16),
            pltpu.VMEM((rows, channels), F32),
            lines,
            pltpu.VMEM((step, 1, seq_len), F32),
            lines, lines,
            dma((2,)), dma((2,)),
            dma((ctx_ways,)), dma((ctx_ways,)), dma((ctx_ways,)), dma((ctx_ways,)),
            dma((ch_ways * outer,)), dma((ch_ways * outer,)),
            dma, dma((outer,)), dma((outer,)), dma((outer,)), dma((inner,)), dma((inner,)),
        ],
        compiler_params=pltpu.CompilerParams(
            collective_id=0, has_side_effects=True, vmem_limit_bytes=48 * 1024 * 1024
        ),
        name="hyena",
    )(value_in, key_in, gate_short, gate_long, taps, long_filter, gains, out_weight)


def solution(mesh):
    in_specs = (
        P("ctx", "ch"),
        P("ctx", "ch"),
        P("ctx", "ch"),
        P("ctx", "ch"),
        P("ch", None),
        P(("ch", "ctx"), None),
        P("ch"),
        P("ctx", "ch"),
    )
    out_specs = P("ctx", "ch")
    return jax.shard_map(shards, mesh=mesh, in_specs=in_specs, out_specs=out_specs, check_vma=False)
```

```python
import functools

import jax
import jax.numpy as jnp
from jax import lax
from jax.experimental import pallas as pl
from jax.experimental.pallas import tpu as pltpu
from jax.sharding import PartitionSpec as P

MESH = pl.DeviceIdType.MESH
F32, BF16 = jnp.float32, jnp.bfloat16


def remote(src, dst, send_sem, recv_sem, ctx, ch=None):
    ch = lax.axis_index("ch") if ch is None else ch
    return pltpu.make_async_remote_copy(
        src_ref=src, dst_ref=dst, send_sem=send_sem, recv_sem=recv_sem, device_id=(ctx, ch), device_id_type=MESH
    )


def short_tile(group_size, own, prior, gate, taps_ref, first_group):
    rows, lanes = own.shape
    tap_count = taps_ref.shape[2]
    row_at = lax.broadcasted_iota(jnp.int32, (rows, tap_count), 0)
    lane_at = lax.broadcasted_iota(jnp.int32, (rows, tap_count), 1)
    before = lane_at > row_at
    window = jnp.concatenate([prior, own], 0)
    group_at = lax.broadcasted_iota(jnp.int32, (rows, lanes), 1) // group_size
    total = jnp.zeros((rows, lanes), F32)
    for group in range(lanes // group_size):
        line = jnp.broadcast_to(taps_ref[first_group + group], (rows, tap_count))
        turned = pltpu.roll(line, 0, 1, stride=1, stride_axis=0)
        band = jnp.concatenate([jnp.where(before, turned, 0.0), jnp.where(before, 0.0, turned)], 1).astype(BF16)
        part = jnp.dot(band, window, preferred_element_type=F32)
        total = jnp.where(group_at == group, part, total)
    return (gate.astype(F32) * total).T


def long_quad(batch, start, xs, hs, gs, skip_ref, skip_at, out):
    _, blocks, width = xs.shape
    half = width // 2
    row_at = lax.broadcasted_iota(jnp.int32, (half, width), 0)
    lane_at = lax.broadcasted_iota(jnp.int32, (half, width), 1)
    after = lane_at >= row_at
    low = lax.broadcasted_iota(jnp.int32, (blocks, width), 1) < half
    first = lax.broadcasted_iota(jnp.int32, (blocks, width), 0) < 1
    deep_at = lax.broadcasted_iota(jnp.int32, (2 * batch, blocks, width), 1)
    signals = [xs[start + c] for c in range(batch)]
    pieces = []
    zero = jnp.zeros((blocks, width), F32)
    for c in range(batch):
        swapped = pltpu.roll(signals[c], half, 1)
        even = signals[c] if c % 2 == 0 else swapped
        odd = swapped if c % 2 == 0 else signals[c]
        keep = low if c % 2 == 0 else jnp.logical_not(low)
        for piece in (even, odd):
            spread = [zero] * (batch // 2)
            spread[c // 2] = jnp.where(keep, piece, 0.0)
            pieces.append(jnp.concatenate(spread, 1))
    left = jnp.concatenate(pieces, 0).astype(BF16)
    previous = [jnp.zeros((half, width), F32)] * batch
    total = jnp.zeros((2 * batch, blocks, width), F32)
    for p in range(blocks):
        rows = []
        for c in range(batch):
            line = jnp.broadcast_to(hs[start + c, :, p * width : (p + 1) * width], (half, width))
            turned = pltpu.roll(line, 0, 1, stride=1, stride_axis=0)
            rows.append(jnp.where(after, turned, previous[c]))
            previous[c] = turned
        right = jnp.concatenate(rows, 0).astype(BF16)
        part = jnp.dot(left, right, preferred_element_type=F32)
        part = part.reshape(2 * batch, blocks, width)
        if p:
            part = jnp.where(deep_at >= p, pltpu.roll(part, p, 1), 0.0)
        total = total + part
    for c in range(batch):
        even, odd = total[2 * c], total[2 * c + 1]
        later = jnp.where(first, 0.0, pltpu.roll(odd, 1, 0))
        result = even + pltpu.roll(jnp.where(low, odd, later), half, 1)
        result = result.astype(BF16).astype(F32)
        gain = jnp.broadcast_to(skip_ref[skip_at + start + c], (blocks, width))
        out[start + c] = gs[start + c] * (result + gain * signals[c])


def kernel(
    sizes,
    value_ref, key_ref, gate_s_ref, gate_l_ref, taps_ref, filt_ref, skip_ref, w_ref,
    out_ref,
    prod, prior, mid_send, gate_send, filt_send, mid_in, gate_in, filt_in, gated, feat, wbuf,
    part_send, part_in, own_part, xs, hs, gs, ys,
    halo_sem, filt_sem, mid_s, mid_r, gate_s, gate_r, feat_s, feat_r, w_own, w_right, w_left, w_recv, part_s, part_r,
):
    ctx_ways, ch_ways, outer, inner, per_dev, group_size = sizes
    rows, channels = value_ref.shape
    me, core = lax.axis_index("ctx"), lax.axis_index("ch")
    line_at, place = me // inner, me % inner

    def owned(d):
        m, g = d // inner, d % inner
        return ch_ways * (inner * (m // ch_ways) + g) + m % ch_ways

    def owner_of(block):
        m_hi, g, e = block // (ch_ways * inner), (block // ch_ways) % inner, block % ch_ways
        return inner * (ch_ways * m_hi + e) + g

    barrier = pltpu.get_barrier_semaphore()

    @pl.loop(1, ctx_ways)
    def _(s):
        pl.semaphore_signal(barrier, inc=1, device_id=((me + s) % ctx_ways, core), device_id_type=MESH)

    for other in range(1, ch_ways):

        @pl.loop(0, outer)
        def _(m):
            pl.semaphore_signal(
                barrier, inc=1, device_id=(m * inner + place, (core + other) % ch_ways), device_id_type=MESH
            )

    prod[...] = (value_ref[...].astype(F32) * key_ref[...].astype(F32)).astype(BF16)
    filt_send[...] = filt_ref[...].astype(BF16)
    pl.semaphore_wait(barrier, ctx_ways - 1 + (ch_ways - 1) * outer)

    halo = remote(prod, prior, halo_sem.at[0], halo_sem.at[1], (me + 1) % ctx_ways)

    @pl.when(me < ctx_ways - 1)
    def _():
        halo.start()

    filt_to = owner_of(me)
    filt_copy = remote(filt_send, filt_in, filt_sem.at[0], filt_sem.at[1], filt_to)

    @pl.when(filt_to != me)
    def _():
        filt_copy.start()

    own_w = pltpu.make_async_copy(w_ref, wbuf.at[line_at], w_own)
    own_w.start()

    def right_copy(s):
        at = jnp.maximum(line_at - s, 0)
        src = w_ref if s == 0 else wbuf.at[at]
        return remote(src, wbuf.at[at], w_right.at[s], w_recv.at[at], (me + inner) % ctx_ways)

    def left_copy(s):
        at = jnp.minimum(line_at + s, outer - 1)
        src = w_ref if s == 0 else wbuf.at[at]
        return remote(src, wbuf.at[at], w_left.at[s], w_recv.at[at], (me + ctx_ways - inner) % ctx_ways)

    def right_on(s):
        return jnp.logical_and(line_at >= s, line_at < outer - 1)

    def left_on(s):
        return jnp.logical_and(line_at + s < outer, line_at > 0)

    def w_step(s):
        @pl.when(right_on(s))
        def _():
            copy = right_copy(s)
            if s:
                copy.wait_recv()
            copy.start()

        @pl.when(left_on(s))
        def _():
            copy = left_copy(s)
            if s:
                copy.wait_recv()
            copy.start()

    w_step(0)

    lanes = min(128, channels)
    in_tile = lanes // per_dev
    tiles = channels // lanes

    def block_copy(buf, into, send, recv, block):
        return remote(buf.at[block], into.at[me], send.at[block], recv.at[me], owner_of(block))

    def send_tile(tile, values, buf, into, send, recv):
        buf[pl.ds(tile * in_tile, in_tile)] = values.reshape(in_tile, per_dev, rows).astype(BF16)
        for b in range(in_tile):
            block = tile * in_tile + b

            @pl.when(owner_of(block) != me)
            def _():
                block_copy(buf, into, send, recv, block).start()

    shift = owned(me) // in_tile

    @pl.loop(0, tiles)
    def _(t):
        tile = (t + shift + 1) % tiles
        at = pl.ds(pl.multiple_of(tile * lanes, lanes), lanes)
        send_tile(tile, gate_l_ref[:, at].astype(F32).T, gate_send, gate_in, gate_s, gate_r)

    @pl.when(me > 0)
    def _():
        halo.wait_recv()

    @pl.when(me == 0)
    def _():
        prior[...] = jnp.zeros_like(prior)

    @pl.loop(0, tiles)
    def _(t):
        tile = (t + shift + 1) % tiles
        at = pl.ds(pl.multiple_of(tile * lanes, lanes), lanes)
        groups = lanes // group_size
        values = short_tile(group_size, prod[:, at], prior[:, at], gate_s_ref[:, at], taps_ref, tile * groups)
        send_tile(tile, values, mid_send, mid_in, mid_s, mid_r)

    mine = owned(me)
    gate_in[me] = gate_send[mine]
    mid_in[me] = mid_send[mine]

    @pl.when(filt_to != me)
    def _():
        filt_copy.wait_recv()

    @pl.when(filt_to == me)
    def _():
        filt_in[...] = filt_send[...]

    @pl.loop(1, ctx_ways)
    def _(s):
        a = (me + s) % ctx_ways
        remote(gate_send.at[0], gate_in.at[a], gate_s.at[0], gate_r.at[a], a).wait_recv()
        remote(mid_send.at[0], mid_in.at[a], mid_s.at[0], mid_r.at[a], a).wait_recv()

    if outer > 2:
        w_step(1)

    step, batch = xs.shape[0], 4

    def long_step(i):
        at = pl.ds(pl.multiple_of(i * step, step), step)
        xs[...] = jnp.swapaxes(mid_in[:, at, :].astype(F32), 0, 1)
        gs[...] = jnp.swapaxes(gate_in[:, at, :].astype(F32), 0, 1)
        hs[...] = filt_in[at, :].astype(F32).reshape(hs.shape)

        @pl.loop(0, step // batch)
        def _(q):
            long_quad(batch, q * batch, xs, hs, gs, skip_ref, i * step, ys)

        gated[:, at, :] = jnp.swapaxes(ys[...], 0, 1).astype(BF16)

    long_steps = per_dev // step
    for s in range(2, outer - 1):
        low, high = (s - 2) * long_steps // (outer - 2), (s - 1) * long_steps // (outer - 2)

        @pl.loop(low, high)
        def _(i):
            long_step(i)

        w_step(s)

    done = (max(outer - 3, 0)) * long_steps // max(outer - 2, 1)

    @pl.loop(done, long_steps)
    def _(i):
        long_step(i)

    slot = core * outer + line_at

    def feat_copy(m, ch, n):
        return remote(
            gated.at[pl.ds(m * inner, inner)], feat.at[slot], feat_s.at[n], feat_r.at[slot], m * inner + place, ch
        )

    for k in range(ch_ways):

        @pl.loop(0, outer)
        def _(s):
            m, ch = (line_at + s) % outer, (core + k) % ch_ways

            @pl.when(jnp.logical_or(m != line_at, ch != core))
            def _():
                feat_copy(m, ch, ch * outer + m).start()

    feat[slot] = gated[pl.ds(me - place, inner)]

    own_w.wait()
    for s in range(1, outer):

        @pl.when(jnp.logical_and(line_at == outer - 1, line_at >= s))
        def _():
            right_copy(s).wait_recv()

        @pl.when(jnp.logical_and(line_at == 0, line_at + s < outer))
        def _():
            left_copy(s).wait_recv()

    @pl.loop(0, ch_ways * outer)
    def _(n):
        @pl.when(n != slot)
        def _():
            remote(
                gated.at[pl.ds(0, inner)], feat.at[n], feat_s.at[n], feat_r.at[n], (n % outer) * inner + place, n // outer
            ).wait_recv()

    depth = ch_ways * outer * per_dev

    def features(g):
        return feat[:, g].astype(F32).reshape(depth, rows).T.astype(BF16)

    cols = min(512, channels)

    @pl.loop(1, inner)
    def _(s):
        g = (place + s) % inner
        left = features(g)

        @pl.loop(0, channels // cols)
        def _(n):
            at = pl.ds(pl.multiple_of(n * cols, cols), cols)
            right = wbuf[:, :, at].reshape(depth, cols)
            part_send[g, :, at] = jnp.dot(left, right, preferred_element_type=F32).astype(BF16)

        remote(part_send.at[g], part_in.at[place], part_s.at[g], part_r.at[place], me - place + g).start()

    left = features(place)

    @pl.loop(0, channels // cols)
    def _(n):
        at = pl.ds(pl.multiple_of(n * cols, cols), cols)
        right = wbuf[:, :, at].reshape(depth, cols)
        own_part[:, at] = jnp.dot(left, right, preferred_element_type=F32)

    @pl.loop(1, inner)
    def _(s):
        g = (place + s) % inner
        remote(part_send.at[g], part_in.at[g], part_s.at[g], part_r.at[g], me - place + g).wait_recv()

        own_part[...] += part_in[g].astype(F32)

    out_ref[...] = own_part[...].astype(BF16)

    @pl.when(me < ctx_ways - 1)
    def _():
        halo.wait_send()

    @pl.when(filt_to != me)
    def _():
        filt_copy.wait_send()

    for s in range(outer - 1):

        @pl.when(right_on(s))
        def _():
            right_copy(s).wait_send()

        @pl.when(left_on(s))
        def _():
            left_copy(s).wait_send()

    @pl.loop(0, ctx_ways)
    def _(block):
        @pl.when(owner_of(block) != me)
        def _():
            block_copy(gate_send, gate_in, gate_s, gate_r, block).wait_send()
            block_copy(mid_send, mid_in, mid_s, mid_r, block).wait_send()

    @pl.loop(0, ch_ways * outer)
    def _(n):
        @pl.when(n != slot)
        def _():
            feat_copy(n % outer, n // outer, n).wait_send()

    @pl.loop(1, inner)
    def _(s):
        g = (place + s) % inner
        remote(part_send.at[g], part_in.at[place], part_s.at[g], part_r.at[place], me - place + g).wait_send()


def shards(
    value_in, key_in, gate_short, gate_long, short_filter, long_filter, skip_gain, out_weight
):
    rows, channels = value_in.shape
    ctx_ways, ch_ways = lax.axis_size("ctx"), lax.axis_size("ch")
    per_dev = channels // ctx_ways
    inner = 2 ** ((ctx_ways.bit_length() - 1) // 2)
    outer = ctx_ways // inner
    group_size = channels // short_filter.shape[0]
    taps = jnp.roll(short_filter[:, ::-1], 1, axis=1).astype(F32)[:, None, :]
    me = lax.axis_index("ctx")
    line_at, place = me // inner, me % inner
    own_block = ch_ways * (inner * (line_at // ch_ways) + place) + line_at % ch_ways
    gains = lax.dynamic_slice_in_dim(skip_gain, own_block * per_dev, per_dev)
    gains = jnp.broadcast_to(gains[:, None, None], (per_dev, 1, rows))
    step = min(16, per_dev)
    seq_len = ctx_ways * rows
    sizes = (ctx_ways, ch_ways, outer, inner, per_dev, group_size)
    blocks = pltpu.VMEM((ctx_ways, per_dev, rows), BF16)
    tokens = pltpu.VMEM((rows, channels), BF16)
    filt = pltpu.VMEM((per_dev, seq_len), BF16)
    lines = pltpu.VMEM((step, ctx_ways, rows), F32)
    dma = pltpu.SemaphoreType.DMA
    vmem = pl.BlockSpec(memory_space=pltpu.VMEM)
    return pl.pallas_call(
        functools.partial(kernel, sizes),
        out_shape=jax.ShapeDtypeStruct((rows, channels), BF16),
        in_specs=[vmem] * 7 + [pl.BlockSpec(memory_space=pl.ANY)],
        out_specs=vmem,
        scratch_shapes=[
            tokens, tokens, blocks, blocks, filt, blocks, blocks, filt, blocks,
            pltpu.VMEM((ch_ways * outer, inner, per_dev, rows), BF16),
            pltpu.VMEM((outer,) + out_weight.shape, BF16),
            pltpu.VMEM((inner, rows, channels), BF16),
            pltpu.VMEM((inner, rows, channels), BF16),
            pltpu.VMEM((rows, channels), F32),
            lines,
            pltpu.VMEM((step, 1, seq_len), F32),
            lines, lines,
            dma((2,)), dma((2,)),
            dma((ctx_ways,)), dma((ctx_ways,)), dma((ctx_ways,)), dma((ctx_ways,)),
            dma((ch_ways * outer,)), dma((ch_ways * outer,)),
            dma, dma((outer,)), dma((outer,)), dma((outer,)), dma((inner,)), dma((inner,)),
        ],
        compiler_params=pltpu.CompilerParams(
            collective_id=0, has_side_effects=True, vmem_limit_bytes=48 * 1024 * 1024
        ),
        name="hyena",
    )(value_in, key_in, gate_short, gate_long, taps, long_filter, gains, out_weight)


def solution(mesh):
    in_specs = (
        P("ctx", "ch"),
        P("ctx", "ch"),
        P("ctx", "ch"),
        P("ctx", "ch"),
        P("ch", None),
        P(("ch", "ctx"), None),
        P("ch"),
        P("ctx", "ch"),
    )
    out_specs = P("ctx", "ch")
    return jax.shard_map(shards, mesh=mesh, in_specs=in_specs, out_specs=out_specs, check_vma=False)
```
